32 devices in a mesh: pix: 16 (over z, y, x), frm: 2 (over core).
Axes of the slice: x: 2, y: 2, z: 4, core: 2. Of those that a mesh axis runs over, the one named last changes fastest.
Arguments:
- curves: bfloat16 [8192, 2048], P('pix', 'frm')
- annulus_of_block: int32 [32], P('pix'), may hold values from 0 to 3, as said below
- ref_blocks: int32 [4, 8], replicated, may hold values from 0 to 31, as said below
- keep_mask: int32 [32, 256], P('pix'), may hold values 0 or 1
- start_basis: bfloat16 [4, 32, 2048], P(None, None, 'frm'), may hold values from -6 to 6
Outputs:
- coefficients: float32 [32, 32, 256], P('pix')
The draws below stay inside these ranges and needn't reach their ends.
Inputs may be any that keep to these rules, and one draw needn't show every extreme that they name: annulus_of_block names every annulus; block b + 16 has the annulus of block b. Every entry of ref_blocks[a, :] is a block of annulus a; each list names the lowest and the highest block of its annulus; entries may repeat.
All inputs are finite; a program needn't handle non-finite values. No bound on the sum of `keep_mask` on one device may be relied on, other than what follows from the above.
Results may differ from the reference program's by a relative error of at most 0.023.
Values may be sent and summed in bfloat16 or wider, within the bound.
No kernel may reach another device: no remote copies, remote signals or barrier semaphores. Data moves between devices by JAX's collectives and lax.ppermute only.
A program may use at most 64 MiB of HBM per device.

```python
import jax
import jax.numpy as jnp
from jax import lax

BLOCK = 256
ANNULI = 4
K = 32
RB = 8
ITERS = 4
NBLK = 32
PIXELS = 8192
FRAMES = 2048


def annulus_table(key):
    half = NBLK // 2
    first = jax.random.randint(jax.random.fold_in(key, 11), (half - ANNULI,), 0, ANNULI)
    second = jax.random.randint(jax.random.fold_in(key, 13), (half - ANNULI,), 0, ANNULI)
    extra = jnp.maximum(first, second).astype(jnp.int32)
    front = jnp.concatenate([jnp.arange(ANNULI, dtype=jnp.int32), extra])
    order = jax.random.permutation(jax.random.fold_in(key, 17), half)
    front = front[order].astype(jnp.int32)
    return jnp.concatenate([front, front])


def draw_annulus_of_block(key, part):
    return annulus_table(key)


def draw_ref_blocks(key, part):
    table = annulus_table(key)
    labels = jnp.arange(ANNULI, dtype=jnp.int32)
    ids = jnp.arange(NBLK, dtype=jnp.int32)
    member = table[None, :] == labels[:, None]
    counts = jnp.sum(member.astype(jnp.int32), axis=1)
    sort_keys = jnp.where(member, ids[None, :], NBLK + ids[None, :]).astype(jnp.int32)
    ordered = jnp.argsort(sort_keys, axis=1, stable=True).astype(jnp.int32)
    offsets = jax.random.randint(jax.random.fold_in(key, 23), (ANNULI, RB - 2), 0, counts[:, None])
    offsets = jnp.concatenate([jnp.zeros((ANNULI, 1), jnp.int32), (counts - 1)[:, None], offsets.astype(jnp.int32)], axis=1)
    return jnp.take_along_axis(ordered, offsets, axis=1).astype(jnp.int32)


def draw_curves(key, part):
    values = jax.random.normal(jax.random.fold_in(key, 43), (PIXELS, FRAMES), jnp.float32)
    return jnp.clip(values, -6.0, 6.0).astype(jnp.bfloat16)


def set_ends(result, stream_key, smallest, largest):
    shape = result.shape
    index_at = [jax.random.randint(jax.random.fold_in(stream_key, axis), (), 0, shape[axis]) for axis in range(len(shape))]
    result = result.at[tuple(index_at)].set(smallest)
    longest = shape.index(max(shape))
    index_at[longest] = (index_at[longest] + 1) % shape[longest]
    return result.at[tuple(index_at)].set(largest)


def block_levels(stream_key, dims, split, low, top_value):
    loudness, own = 1.0, jax.random.fold_in(stream_key, 6)
    for axis_at, blocks in split:
        steps = jnp.exp(jax.random.uniform(jax.random.fold_in(own, axis_at), (blocks,), jnp.float32, low / len(split), top_value / len(split)))
        loudness = loudness * jnp.repeat(steps, dims[axis_at] // blocks).reshape([-1 if axis == axis_at else 1 for axis in range(len(dims))])
    return loudness


def centred(key, shape, spread, most, split=(), kind=jnp.bfloat16):
    array = jax.random.normal(key, shape, jnp.float32) * spread
    if len(split) > 0:
        array = block_levels(key, shape, split, -0.22, 0.18) * array
    return jnp.clip(array, min=-most, max=most).astype(kind)


def setup_inputs(seed: int = 0) -> dict:
    seeds = jax.random.split(jax.random.key(seed), 6)
    return {
        "curves": draw_curves(jax.random.fold_in(seeds[5], 71), 0),
        "annulus_of_block": draw_annulus_of_block(jax.random.fold_in(seeds[5], 71), 0),
        "ref_blocks": draw_ref_blocks(jax.random.fold_in(seeds[5], 71), 0),
        "keep_mask": set_ends((jax.random.randint(seeds[3], (NBLK, BLOCK), 0, 8) < 7).astype(jnp.int32), jax.random.fold_in(seeds[3], 1), 0, 1),
        "start_basis": centred(seeds[4], (ANNULI, K, FRAMES), 1.0, 6.0, ((2, 2),)),
    }


def project_all(blocks, annulus_of_block, basis_bf):

    def one_block(pair):
        block_rows, label = pair
        chosen = basis_bf[label]
        return jnp.dot(chosen.astype(jnp.float32), block_rows.T.astype(jnp.float32), preferred_element_type=jnp.float32)
    return lax.map(one_block, (blocks, annulus_of_block))

def reference(curves, annulus_of_block, ref_blocks, keep_mask, start_basis):
    blocks = curves.reshape(NBLK, BLOCK, FRAMES)
    labels = jnp.arange(ANNULI, dtype=jnp.int32)
    member = annulus_of_block[:, None] == labels[None, :]
    global_ids = jnp.arange(NBLK, dtype=jnp.int32)
    listed = jnp.any((ref_blocks[None, :, :] == global_ids[:, None, None]) & member[:, :, None], axis=(1, 2))
    weight = (listed[:, None] & (keep_mask == 1)).astype(jnp.float32)
    basis_bf = start_basis
    for step in range(ITERS):
        proj = project_all(blocks, annulus_of_block, basis_bf) * weight[:, None, :]
        proj_bf = proj.astype(jnp.bfloat16)

        def accumulate(total, triple):
            block_rows, weights_bf, label = triple
            term = jnp.dot(weights_bf.astype(jnp.float32), block_rows.astype(jnp.float32), preferred_element_type=jnp.float32)
            return (total.at[label].add(term), None)
        span, unused = lax.scan(accumulate, jnp.zeros((ANNULI, K, FRAMES), jnp.float32), (blocks, proj_bf, annulus_of_block))
        gram = jnp.einsum('akf,ajf->akj', span, span, precision=lax.Precision.HIGHEST)
        lower = jnp.linalg.cholesky(gram)
        ortho = lax.linalg.triangular_solve(lower, span, left_side=True, lower=True)
        basis_bf = ortho.astype(jnp.bfloat16)
    return project_all(blocks, annulus_of_block, basis_bf)
```

```python
import functools

import jax
import jax.numpy as jnp
from jax import lax
from jax.experimental import pallas as pl
from jax.experimental.pallas import tpu as pltpu
from jax.sharding import PartitionSpec as P

ITERS = 4
LANES = 128
BOTH = ("pix", "frm")
EXACT = lax.Precision.HIGHEST


def inverse_factor(gram):
    k = gram.shape[0]
    rows = lax.broadcasted_iota(jnp.int32, (k, LANES), 0)
    cols = lax.broadcasted_iota(jnp.int32, (k, LANES), 1)
    wide = jnp.concatenate([gram, jnp.zeros((k, LANES - k), jnp.float32)], axis=1)
    wide = wide + jnp.where(cols == rows + k, 1.0, 0.0)
    for step in range(k - 1):
        pivot_row = wide[step : step + 1, :]
        scaled = pivot_row / pivot_row[:, step : step + 1]
        factor = jnp.where(rows > step, jnp.broadcast_to(wide[:, step : step + 1], (k, LANES)), 0.0)
        wide = wide - factor * scaled
    pivots = jnp.sum(jnp.where(cols == rows, wide, 0.0), axis=1, keepdims=True)
    return wide[:, k : 2 * k] * lax.rsqrt(pivots)


def load_curves(frm, own_ref, got_refs, held, sems):
    chunk, frames = held.shape
    width = own_ref.shape[1]
    others = len(got_refs) + 1
    copies = [
        pltpu.make_async_copy(
            own_ref.at[pl.ds(frm * chunk, chunk)],
            held.at[:, pl.ds(pl.multiple_of(frm * width, LANES), width)],
            sems.at[0],
        )
    ]
    for shift, got in enumerate(got_refs, 1):
        source = lax.rem(frm - shift + others, others)
        copies.append(
            pltpu.make_async_copy(
                got.at[pl.ds(0, chunk)],
                held.at[:, pl.ds(pl.multiple_of(source * width, LANES), width)],
                sems.at[shift],
            )
        )
    for copy in copies:
        copy.start()
    return copies


def project(basis, held):
    return lax.dot_general(
        basis, held[...], (((1,), (1,)), ((), ())), preferred_element_type=jnp.float32
    )


def store_span(proj, weight, held, out_ref):
    proj_bf = (proj * weight).astype(jnp.bfloat16)
    span = jnp.dot(proj_bf, held[...], preferred_element_type=jnp.float32)
    parts, rows = out_ref.shape[0], 32 * held.shape[1] // LANES // out_ref.shape[0]
    across = held.shape[1] // LANES
    for j in range(parts):
        top, left = j // across * rows, j % across * LANES
        out_ref[j, :rows, :] = span[top : top + rows, left : left + LANES].astype(out_ref.dtype)


def first_kernel(others, pos_ref, ann_ref, own_ref, start_ref, weight_ref, *refs):
    got_refs, (out_ref, held, basis, sems) = refs[: others - 1], refs[others - 1 :]
    frm, label = pos_ref[0], ann_ref[0]
    chunk = held.shape[0]
    width = own_ref.shape[1]
    copies = load_curves(frm, own_ref, got_refs, held, sems)
    copies.append(
        pltpu.make_async_copy(
            start_ref.at[label],
            basis.at[:, pl.ds(pl.multiple_of(frm * width, LANES), width)],
            sems.at[others],
        )
    )
    copies[-1].start()
    for shift, got in enumerate(got_refs, 1):
        source = lax.rem(frm - shift + others, others)
        copies.append(
            pltpu.make_async_copy(
                got.at[pl.ds(chunk, basis.shape[0])],
                basis.at[:, pl.ds(pl.multiple_of(source * width, LANES), width)],
                sems.at[others + shift],
            )
        )
        copies[-1].start()
    rows = out_ref.shape[1] - 8
    mark = jnp.full((8, LANES), label, jnp.int32).astype(jnp.float32)
    for j in range(out_ref.shape[0]):
        out_ref[j, rows:, :] = mark
    for copy in copies:
        copy.wait()
    store_span(project(basis[...], held), weight_ref[...], held, out_ref)


def step_kernel(others, last, pos_ref, span_ref, own_ref, weight_ref, *refs):
    got_refs, (out_ref, held, whole, sems) = refs[: others - 1], refs[others - 1 :]
    copies = load_curves(pos_ref[0], own_ref, got_refs, held, sems)
    parts, rows = span_ref.shape[:2]
    across = held.shape[1] // LANES
    for j in range(parts):
        top, left = j // across * rows, j % across * LANES
        whole[top : top + rows, left : left + LANES] = span_ref[j].astype(jnp.float32)
    span = whole[...]
    gram = lax.dot_general(
        span, span, (((1,), (1,)), ((), ())), precision=EXACT, preferred_element_type=jnp.float32
    )
    ortho = jnp.dot(
        inverse_factor(gram), span, precision=EXACT, preferred_element_type=jnp.float32
    )
    basis = ortho.astype(jnp.bfloat16)
    for copy in copies:
        copy.wait()
    proj = project(basis, held)
    if last:
        out_ref[...] = proj
    else:
        store_span(proj, weight_ref[...], held, out_ref)


def sum_kernel(annuli, first, in_ref, *refs):
    parts, rows = in_ref.shape[0], refs[0].shape[1]
    if first:
        out_ref, mark_ref = refs
        for j in range(parts):
            mark_ref[j : j + 1, :] = in_ref[j, rows : rows + 1, :]
    else:
        mark_ref, out_ref = refs
        rows = out_ref.shape[1]

    def add(j, sums):
        part = in_ref[j, :rows, :].astype(jnp.float32)
        mark = mark_ref[pl.ds(j, 1), :]
        return tuple(s + jnp.where(mark == a, part, 0.0) for a, s in enumerate(sums))

    def give(j, sums):
        mark = mark_ref[pl.ds(j, 1), :]
        total = sums[0]
        for a in range(1, annuli):
            total = jnp.where(mark == a, sums[a], total)
        out_ref[j] = total.astype(out_ref.dtype)

    sums = tuple(jnp.zeros((rows, LANES), jnp.float32) for _ in range(annuli))
    if parts <= 32:
        for j in range(parts):
            sums = add(j, sums)
        for j in range(parts):
            give(j, sums)
    else:
        sums = lax.fori_loop(0, parts, add, sums)
        lax.fori_loop(0, parts, lambda j, c: (give(j, sums), c)[1], 0)


def shards(npix, nfrm, curves, annulus_of_block, ref_blocks, keep_mask, start_basis):
    pixels, width = curves.shape
    nblocks, block = keep_mask.shape
    annuli, comps, _ = start_basis.shape
    chunk, frames, parts = pixels // nfrm, width * nfrm, npix * nfrm
    rows = comps * frames // LANES // parts
    pix, frm = lax.axis_index("pix"), lax.axis_index("frm")

    def label_at(place):
        return annulus_of_block[place * chunk // block]

    got = []
    for shift in range(1, nfrm):
        target = lax.rem(frm + shift, nfrm)
        message = jnp.concatenate(
            [
                lax.dynamic_slice_in_dim(curves, target * chunk, chunk, 0),
                lax.dynamic_index_in_dim(start_basis, label_at(target), 0, keepdims=False),
            ]
        )
        got.append(lax.ppermute(message, "frm", [(i, (i + shift) % nfrm) for i in range(nfrm)]))

    label = label_at(frm)
    mine = pix * nblocks + frm * chunk // block
    listed = jnp.any(lax.dynamic_index_in_dim(ref_blocks, label, 0) == mine)
    kept = lax.dynamic_slice_in_dim(keep_mask.reshape(1, pixels), frm * chunk, chunk, 1)
    weight = (listed & (kept == 1)).astype(jnp.float32)
    position = frm.reshape(1)

    smem = pl.BlockSpec(memory_space=pltpu.SMEM)
    vmem = pl.BlockSpec(memory_space=pltpu.VMEM)
    anyw = pl.BlockSpec(memory_space=pl.ANY)
    shape = jax.ShapeDtypeStruct
    held = pltpu.VMEM((chunk, frames), jnp.bfloat16)
    params = pltpu.CompilerParams(vmem_limit_bytes=32 * 1024 * 1024)

    sent = pl.pallas_call(
        functools.partial(first_kernel, nfrm),
        out_shape=shape((parts, rows + 8, LANES), jnp.float32),
        in_specs=[smem, smem, anyw, anyw, vmem] + [anyw] * (nfrm - 1),
        out_specs=vmem,
        scratch_shapes=[
            held,
            pltpu.VMEM((comps, frames), jnp.bfloat16),
            pltpu.SemaphoreType.DMA((2 * nfrm,)),
        ],
        compiler_params=params,
        name="first_span",
    )(position, label.reshape(1), curves, start_basis, weight, *got)

    marks = None
    for step in range(ITERS):
        kind = jnp.float32
        taken = lax.all_to_all(sent, BOTH, 0, 0, tiled=True)
        total_shape = shape((parts, rows, LANES), kind)
        if step == 0:
            total, marks = pl.pallas_call(
                functools.partial(sum_kernel, annuli, True),
                out_shape=(total_shape, shape((parts, LANES), jnp.float32)),
                in_specs=[vmem],
                out_specs=(vmem, vmem),
                compiler_params=params,
                name="sum_first",
            )(taken)
        else:
            total = pl.pallas_call(
                functools.partial(sum_kernel, annuli, False),
                out_shape=total_shape,
                in_specs=[vmem, vmem],
                out_specs=vmem,
                compiler_params=params,
                name="sum_spans",
            )(taken, marks)
        span = lax.all_to_all(total, BOTH, 0, 0, tiled=True)
        last = step == ITERS - 1
        sent = pl.pallas_call(
            functools.partial(step_kernel, nfrm, last),
            out_shape=shape((comps, chunk) if last else (parts, rows, LANES), jnp.float32),
            in_specs=[smem, vmem, anyw, vmem] + [anyw] * (nfrm - 1),
            out_specs=vmem,
            scratch_shapes=[
                held,
                pltpu.VMEM((comps, frames), jnp.float32),
                pltpu.SemaphoreType.DMA((nfrm,)),
            ],
            compiler_params=params,
            name="fit" if last else "step",
        )(position, span, curves, weight, *got)

    if nfrm == 2 and chunk == block:
        other = lax.ppermute(sent, "frm", [(0, 1), (1, 0)])
        low, high = jnp.where(frm == 0, sent, other), jnp.where(frm == 0, other, sent)
        return jnp.stack([low, high])
    every = lax.all_gather(sent, "frm")
    return every.swapaxes(0, 1).reshape(comps, nblocks, block).swapaxes(0, 1)


def solution(mesh):
    in_specs = (P("pix", "frm"), P("pix"), P(), P("pix", None), P(None, None, "frm"))
    out_specs = P("pix", None, None)
    body = functools.partial(shards, mesh.shape["pix"], mesh.shape["frm"])
    return jax.shard_map(body, mesh=mesh, in_specs=in_specs, out_specs=out_specs, check_vma=False)
```

```python
import functools

import jax
import jax.numpy as jnp
from jax import lax
from jax.experimental import pallas as pl
from jax.experimental.pallas import tpu as pltpu
from jax.sharding import PartitionSpec as P

ITERS = 4
LANES = 128
PANEL = 16
BOTH = ("pix", "frm")
EXACT = lax.Precision.HIGHEST
ROWS_TO_ROWS = (((1,), (1,)), ((), ()))


def inverse_factor(gram):
    k = gram.shape[0]
    rows = lax.broadcasted_iota(jnp.int32, (k, LANES), 0)
    cols = lax.broadcasted_iota(jnp.int32, (k, LANES), 1)
    wide = jnp.concatenate([gram, jnp.zeros((k, LANES - k), jnp.float32)], axis=1)
    wide = wide + jnp.where(cols == rows + k, 1.0, 0.0)
    for base in range(0, k, PANEL):
        low, below = wide[base:, :], rows[base:, :]
        panel = [jnp.broadcast_to(low[:, base + j : base + j + 1], low.shape) for j in range(PANEL)]
        for j in range(PANEL):
            factor = jnp.where(below > base + j, panel[j] * (1.0 / panel[j][j : j + 1, :]), 0.0)
            for i in range(j + 1, PANEL):
                panel[i] = panel[i] - factor * panel[i][j : j + 1, :]
            low = low - factor * low[j : j + 1, :]
        wide = jnp.concatenate([wide[:base, :], low], axis=0) if base else low
    pivots = jnp.sum(jnp.where(cols == rows, wide, 0.0), axis=1, keepdims=True)
    return wide[:, k : 2 * k] * lax.rsqrt(pivots)


def pieces(wide):
    high = wide.astype(jnp.bfloat16)
    rest = wide - high.astype(jnp.float32)
    middle = rest.astype(jnp.bfloat16)
    low = (rest - middle.astype(jnp.float32)).astype(jnp.bfloat16)
    return jnp.concatenate([high, middle, low], axis=0)


def fold(stacked, k):
    return (stacked[2 * k :] + stacked[k : 2 * k]) + stacked[:k]


def dot_rows(left, right):
    return lax.dot_general(left, right, ROWS_TO_ROWS, preferred_element_type=jnp.float32)


def tiles(parts, rows, across):
    for j in range(parts):
        yield j, pl.ds(j // across * rows, rows), pl.ds(j % across * LANES, LANES)


def store_span(span, out_ref):
    parts, rows = out_ref.shape[:2]
    for j, down, along in tiles(parts, rows, span.shape[1] // LANES):
        out_ref[j] = lax.slice(
            span, (down.start, along.start), (down.start + rows, along.start + LANES)
        ).astype(out_ref.dtype)


def wait_all(copies):
    for copy in copies:
        copy.start()
    for copy in copies:
        copy.wait()


def pack_kernel(chunk, block, others, ann_ref, own_ref, start_ref, *refs):
    out_refs, sems = refs[:-1], refs[-1]
    frm = lax.axis_index("frm")
    copies = []
    for shift, out_ref in enumerate(out_refs, 1):
        target = lax.rem(frm + shift, others)
        label = ann_ref[target * chunk // block]
        copies += [
            pltpu.make_async_copy(
                own_ref.at[pl.ds(pl.multiple_of(target * chunk, chunk), chunk)],
                out_ref.at[pl.ds(0, chunk)],
                sems.at[2 * shift - 2],
            ),
            pltpu.make_async_copy(
                start_ref.at[label],
                out_ref.at[pl.ds(chunk, start_ref.shape[1])],
                sems.at[2 * shift - 1],
            ),
        ]
    wait_all(copies)


def first_kernel(block, others, ann_ref, listed_ref, keep_ref, own_ref, start_ref, *refs):
    got_refs = refs[: others - 1]
    out_ref, held, weight_ref, basis, sems = refs[others - 1 :]
    pix, frm = lax.axis_index("pix"), lax.axis_index("frm")
    chunk, width = held.shape[0], own_ref.shape[1]
    place = frm * chunk // block
    label = ann_ref[place]
    copies = []
    for shift in range(others):
        source = lax.rem(frm - shift + others, others)
        along = pl.ds(pl.multiple_of(source * width, LANES), width)
        if shift:
            curves = got_refs[shift - 1].at[pl.ds(0, chunk)]
            start = got_refs[shift - 1].at[pl.ds(chunk, basis.shape[0])]
        else:
            curves = own_ref.at[pl.ds(pl.multiple_of(frm * chunk, chunk), chunk)]
            start = start_ref.at[label]
        copies += [
            pltpu.make_async_copy(curves, held.at[:, along], sems.at[2 * shift]),
            pltpu.make_async_copy(start, basis.at[:, along], sems.at[2 * shift + 1]),
        ]
    for copy in copies:
        copy.start()
    mine = pix * ann_ref.shape[0] + place
    listed = listed_ref[label, 0] == mine
    for entry in range(1, listed_ref.shape[1]):
        listed = listed | (listed_ref[label, entry] == mine)
    listed = listed.astype(jnp.int32)
    kept = keep_ref[pl.ds(frm, 1), :]
    weight = jnp.where(kept == 1, listed, 0).astype(jnp.float32)
    weight_ref[...] = weight
    for copy in copies:
        copy.wait()
    proj_bf = (dot_rows(basis[...], held[...]) * weight).astype(jnp.bfloat16)
    span = jnp.dot(proj_bf, held[...], preferred_element_type=jnp.float32)
    store_span(span + ((1 - listed) * label).astype(jnp.float32), out_ref)


def step_kernel(last, span_ref, held, weight_ref, out_ref, whole):
    parts, rows = span_ref.shape[:2]
    for j, down, along in tiles(parts, rows, held.shape[1] // LANES):
        whole[down, along] = span_ref[j]
    span = whole[...]
    comps = span.shape[0]
    if span.dtype == jnp.bfloat16:
        gram = dot_rows(span, span)
        raw = dot_rows(span, held[...])
    else:
        gram = lax.dot_general(
            span, span, ROWS_TO_ROWS, precision=EXACT, preferred_element_type=jnp.float32
        )
        raw = fold(dot_rows(pieces(span), held[...]), comps)
    proj = jnp.dot(inverse_factor(gram), raw, precision=EXACT, preferred_element_type=jnp.float32)
    if last:
        out_ref[...] = proj
    else:
        proj_bf = (proj * weight_ref[...]).astype(jnp.bfloat16)
        store_span(jnp.dot(proj_bf, held[...], preferred_element_type=jnp.float32), out_ref)


def add_and_give(annuli, in_ref, mark_ref, give_ref, out_ref):
    parts, rows = out_ref.shape[:2]

    def add(j, sums):
        part = in_ref[j].astype(jnp.float32)
        mark = mark_ref[pl.ds(j, 1), :]
        return tuple(s + jnp.where(mark == a, part, 0.0) for a, s in enumerate(sums))

    def give(j, sums):
        mark = give_ref[pl.ds(j, 1), :]
        total = sums[0]
        for a in range(1, annuli):
            total = jnp.where(mark == a, sums[a], total)
        out_ref[j] = total.astype(out_ref.dtype)
        return sums

    sums = tuple(jnp.zeros((rows, LANES), jnp.float32) for _ in range(annuli))
    if parts <= 32:
        for j in range(parts):
            sums = add(j, sums)
        for j in range(parts):
            give(j, sums)
    else:
        sums = lax.fori_loop(0, parts, add, sums)
        lax.fori_loop(0, parts, give, sums)


def first_sum_kernel(annuli, chunks, listed_ref, in_ref, out_ref, give_ref, mark_ref, table):
    parts = in_ref.shape[0]
    blocks = table.shape[0]
    for b in range(blocks):
        table[b] = -1
    for a in range(annuli):
        for entry in range(listed_ref.shape[1]):
            table[listed_ref[a, entry]] = a
    for j in range(parts):
        label = jnp.full((1, LANES), table[j // chunks], jnp.int32)
        said = in_ref[j, :1, :].astype(jnp.int32)
        mark_ref[j : j + 1, :] = label
        give_ref[j : j + 1, :] = jnp.where(label < 0, said, label)
    add_and_give(annuli, in_ref, mark_ref, give_ref, out_ref)


def sum_kernel(annuli, in_ref, give_ref, out_ref):
    add_and_give(annuli, in_ref, give_ref, give_ref, out_ref)


def shards(npix, nfrm, curves, annulus_of_block, ref_blocks, keep_mask, start_basis):
    pixels, width = curves.shape
    nblocks, block = keep_mask.shape
    annuli, comps, _ = start_basis.shape
    chunk, frames, parts = pixels // nfrm, width * nfrm, npix * nfrm
    rows = comps * frames // LANES // parts
    narrow = jnp.bfloat16 if rows % 16 == 0 else jnp.float32

    smem = pl.BlockSpec(memory_space=pltpu.SMEM)
    vmem = pl.BlockSpec(memory_space=pltpu.VMEM)
    anyw = pl.BlockSpec(memory_space=pl.ANY)
    shape = jax.ShapeDtypeStruct

    def call(kernel, out, ins, outs, name, scratch=()):
        return pl.pallas_call(
            kernel,
            out_shape=out,
            in_specs=ins,
            out_specs=outs,
            scratch_shapes=list(scratch),
            compiler_params=pltpu.CompilerParams(vmem_limit_bytes=32 * 1024 * 1024),
            name=name,
        )

    messages = call(
        functools.partial(pack_kernel, chunk, block, nfrm),
        [shape((chunk + comps, width), jnp.bfloat16)] * (nfrm - 1),
        [smem, anyw, anyw],
        [vmem] * (nfrm - 1),
        "pack",
        [pltpu.SemaphoreType.DMA((2 * nfrm - 2,))],
    )(annulus_of_block, curves, start_basis)
    got = [
        lax.ppermute(message, "frm", [(i, (i + shift) % nfrm) for i in range(nfrm)])
        for shift, message in enumerate(messages, 1)
    ]
    sent, held, weight = call(
        functools.partial(first_kernel, block, nfrm),
        (
            shape((parts, rows, LANES), jnp.float32),
            shape((chunk, frames), jnp.bfloat16),
            shape((1, chunk), jnp.float32),
        ),
        [smem, smem, vmem] + [anyw] * (nfrm + 1),
        (vmem, vmem, vmem),
        "first_span",
        [pltpu.VMEM((comps, frames), jnp.bfloat16), pltpu.SemaphoreType.DMA((2 * nfrm,))],
    )(annulus_of_block, ref_blocks, keep_mask.reshape(nfrm, chunk), curves, start_basis, *got)

    give = None
    for step in range(ITERS):
        kind = narrow if step else jnp.float32
        taken = lax.all_to_all(sent, BOTH, 0, 0, tiled=True)
        total = shape((parts, rows, LANES), kind)
        if step == 0:
            total, give = call(
                functools.partial(first_sum_kernel, annuli, parts // (npix * nblocks)),
                (total, shape((parts, LANES), jnp.int32)),
                [smem, vmem],
                (vmem, vmem),
                "first_sum",
                [
                    pltpu.VMEM((parts, LANES), jnp.int32),
                    pltpu.SMEM((npix * nblocks,), jnp.int32),
                ],
            )(ref_blocks, taken)
        else:
            total = call(
                functools.partial(sum_kernel, annuli), total, [vmem, vmem], vmem, "sum"
            )(taken, give)
        span = lax.all_to_all(total, BOTH, 0, 0, tiled=True)
        last = step == ITERS - 1
        sent = call(
            functools.partial(step_kernel, last),
            shape((comps, chunk), jnp.float32) if last else shape((parts, rows, LANES), narrow),
            [vmem, vmem, vmem],
            vmem,
            "fit" if last else "step",
            [pltpu.VMEM((comps, frames), kind)],
        )(span, held, weight)

    if nfrm == 2 and chunk == block:
        frm = lax.axis_index("frm")
        other = lax.ppermute(sent, "frm", [(0, 1), (1, 0)])
        return jnp.stack([jnp.where(frm == 0, sent, other), jnp.where(frm == 0, other, sent)])
    every = lax.all_gather(sent, "frm")
    return every.swapaxes(0, 1).reshape(comps, nblocks, block).swapaxes(0, 1)


def solution(mesh):
    in_specs = (P("pix", "frm"), P("pix"), P(), P("pix", None), P(None, None, "frm"))
    out_specs = P("pix", None, None)
    body = functools.partial(shards, mesh.shape["pix"], mesh.shape["frm"])
    return jax.shard_map(body, mesh=mesh, in_specs=in_specs, out_specs=out_specs, check_vma=False)
```

```python
import functools

import jax
import jax.numpy as jnp
from jax import lax
from jax.experimental import pallas as pl
from jax.experimental.pallas import tpu as pltpu
from jax.sharding import PartitionSpec as P

ITERS = 4
LANES = 128
PANEL = 16
BOTH = ("pix", "frm")
EXACT = lax.Precision.HIGHEST
ROWS_TO_ROWS = (((1,), (1,)), ((), ()))


def inverse_factor(gram):
    k = gram.shape[0]
    rows = lax.broadcasted_iota(jnp.int32, (k, LANES), 0)
    cols = lax.broadcasted_iota(jnp.int32, (k, LANES), 1)
    wide = jnp.concatenate([gram, jnp.zeros((k, LANES - k), jnp.float32)], axis=1)
    wide = wide + jnp.where(cols == rows + k, 1.0, 0.0)
    for base in range(0, k, PANEL):
        low, below = wide[base:, :], rows[base:, :]
        panel = [jnp.broadcast_to(low[:, base + j : base + j + 1], low.shape) for j in range(PANEL)]
        for j in range(PANEL):
            factor = jnp.where(below > base + j, panel[j] * (1.0 / panel[j][j : j + 1, :]), 0.0)
            for i in range(j + 1, PANEL):
                panel[i] = panel[i] - factor * panel[i][j : j + 1, :]
            low = low - factor * low[j : j + 1, :]
        wide = jnp.concatenate([wide[:base, :], low], axis=0) if base else low
    pivots = jnp.sum(jnp.where(cols == rows, wide, 0.0), axis=1, keepdims=True)
    return wide[:, k : 2 * k] * lax.rsqrt(pivots)


def pieces(wide):
    high = wide.astype(jnp.bfloat16)
    rest = wide - high.astype(jnp.float32)
    middle = rest.astype(jnp.bfloat16)
    low = (rest - middle.astype(jnp.float32)).astype(jnp.bfloat16)
    return jnp.concatenate([high, middle, low], axis=0)


def fold(stacked, k):
    return (stacked[2 * k :] + stacked[k : 2 * k]) + stacked[:k]


def dot_rows(left, right):
    return lax.dot_general(left, right, ROWS_TO_ROWS, preferred_element_type=jnp.float32)


def store_tiles(span, first, across, out_ref):
    rows = out_ref.shape[1]
    for down in range(span.shape[0] // rows):
        for along in range(span.shape[1] // LANES):
            tile = span[down * rows : (down + 1) * rows, along * LANES : (along + 1) * LANES]
            out_ref[first + (down * across + along)] = tile.astype(out_ref.dtype)


def span_of(proj, weight, held, sources, out_ref):
    proj_bf = (proj * weight).astype(jnp.bfloat16)
    width = held[0].shape[1] // LANES
    for curves, source in zip(held, sources):
        span = jnp.dot(proj_bf, curves[...], preferred_element_type=jnp.float32)
        yield span, source * width, width * len(held)


def frame_order(others):
    frm = lax.axis_index("frm")
    return [lax.rem(frm - shift + others, others) for shift in range(others)]


def pack_kernel(own_ref, *refs):
    out_refs, sems = refs[:-1], refs[-1]
    others = len(out_refs) + 1
    chunk = out_refs[0].shape[0]
    copies = []
    for shift, out_ref in enumerate(out_refs, 1):
        target = lax.rem(lax.axis_index("frm") + shift, others)
        rows = pl.ds(pl.multiple_of(target * chunk, chunk), chunk)
        copies.append(pltpu.make_async_copy(own_ref.at[rows], out_ref, sems.at[shift - 1]))
    for copy in copies:
        copy.start()
    for copy in copies:
        copy.wait()


def own_kernel(
    block, chunks, ann_ref, listed_ref, keep_ref, all_ref, start_ref,
    own_ref, raw_ref, weight_ref, say_ref, mark_ref, basis, table, sems,
):
    pix, frm = lax.axis_index("pix"), lax.axis_index("frm")
    chunk = own_ref.shape[0]
    rows = pl.ds(pl.multiple_of(frm * chunk, chunk), chunk)
    place = frm * chunk // block
    label = ann_ref[place]
    curves = pltpu.make_async_copy(all_ref.at[rows], own_ref, sems.at[0])
    start = pltpu.make_async_copy(start_ref.at[label], basis, sems.at[1])
    curves.start()
    start.start()
    for b in range(table.shape[0]):
        table[b] = -1
    for a in range(listed_ref.shape[0]):
        for entry in range(listed_ref.shape[1]):
            table[listed_ref[a, entry]] = a
    for j in range(mark_ref.shape[0]):
        mark_ref[j : j + 1, :] = jnp.full((1, LANES), table[j // chunks], jnp.int32)
    listed = (table[pix * ann_ref.shape[0] + place] >= 0).astype(jnp.int32)
    kept = keep_ref[pl.ds(frm, 1), :]
    weight_ref[...] = jnp.where(kept == 1, listed, 0).astype(jnp.float32)
    say_ref[...] = jnp.full((1, LANES), (1 - listed) * label, jnp.int32).astype(jnp.float32)
    curves.wait()
    start.wait()
    raw_ref[...] = dot_rows(basis[...], own_ref[...])


def first_kernel(block, others, ann_ref, raw_ref, weight_ref, say_ref, own_ref, *refs):
    got, starts, out_ref = refs[: others - 1], refs[others - 1 : -1], refs[-1]
    label = ann_ref[lax.axis_index("frm") * own_ref.shape[0] // block]
    proj = raw_ref[...]
    for curves, start in zip(got, starts):
        proj = proj + dot_rows(start[label], curves[...])
    held, weight = (own_ref, *got), weight_ref[...]
    for span, first, across in span_of(proj, weight, held, frame_order(others), out_ref):
        store_tiles(
            jnp.concatenate(
                [
                    span[:, i : i + LANES] + say_ref[...]
                    for i in range(0, span.shape[1], LANES)
                ],
                axis=1,
            ),
            first,
            across,
            out_ref,
        )


def step_kernel(last, others, span_ref, weight_ref, *refs):
    held, (out_ref, whole) = refs[:others], refs[others:]
    parts, rows = span_ref.shape[:2]
    comps, frames = whole.shape
    across, width = frames // LANES, frames // others
    for j in range(parts):
        down, along = j // across * rows, j % across * LANES
        whole[down : down + rows, along : along + LANES] = span_ref[j]
    span, sources = whole[...], frame_order(others)
    raw = jnp.zeros((comps, held[0].shape[0]), jnp.float32)
    for curves, source in zip(held, sources):
        part = whole[:, pl.ds(pl.multiple_of(source * width, LANES), width)]
        if span.dtype == jnp.bfloat16:
            raw = raw + dot_rows(part, curves[...])
        else:
            raw = raw + fold(dot_rows(pieces(part), curves[...]), comps)
    if span.dtype == jnp.bfloat16:
        gram = dot_rows(span, span)
    else:
        gram = lax.dot_general(
            span, span, ROWS_TO_ROWS, precision=EXACT, preferred_element_type=jnp.float32
        )
    proj = jnp.dot(inverse_factor(gram), raw, precision=EXACT, preferred_element_type=jnp.float32)
    if last:
        out_ref[...] = proj
    else:
        for span, first, across in span_of(proj, weight_ref[...], held, sources, out_ref):
            store_tiles(span, first, across, out_ref)


def place_kernel(own_ref, other_ref, out_ref, sems):
    frm = lax.axis_index("frm")
    copies = [
        pltpu.make_async_copy(own_ref, out_ref.at[frm], sems.at[0]),
        pltpu.make_async_copy(other_ref, out_ref.at[1 - frm], sems.at[1]),
    ]
    for copy in copies:
        copy.start()
    for copy in copies:
        copy.wait()


def add_and_give(annuli, in_ref, mark_ref, give_ref, out_ref):
    parts, rows = out_ref.shape[:2]

    def add(j, sums):
        part = in_ref[j].astype(jnp.float32)
        mark = mark_ref[pl.ds(j, 1), :]
        return tuple(s + jnp.where(mark == a, part, 0.0) for a, s in enumerate(sums))

    def give(j, sums):
        mark = give_ref[pl.ds(j, 1), :]
        total = sums[0]
        for a in range(1, annuli):
            total = jnp.where(mark == a, sums[a], total)
        out_ref[j] = total.astype(out_ref.dtype)
        return sums

    sums = tuple(jnp.zeros((rows, LANES), jnp.float32) for _ in range(annuli))
    if parts <= 32:
        for j in range(parts):
            sums = add(j, sums)
        for j in range(parts):
            give(j, sums)
    else:
        sums = lax.fori_loop(0, parts, add, sums)
        lax.fori_loop(0, parts, give, sums)


def first_sum_kernel(annuli, in_ref, mark_ref, out_ref, give_ref):
    for j in range(in_ref.shape[0]):
        label = mark_ref[j : j + 1, :]
        said = in_ref[j, :1, :].astype(jnp.int32)
        give_ref[j : j + 1, :] = jnp.where(label < 0, said, label)
    add_and_give(annuli, in_ref, mark_ref, give_ref, out_ref)


def sum_kernel(annuli, in_ref, give_ref, out_ref):
    add_and_give(annuli, in_ref, give_ref, give_ref, out_ref)


def shards(npix, nfrm, curves, annulus_of_block, ref_blocks, keep_mask, start_basis):
    pixels, width = curves.shape
    nblocks, block = keep_mask.shape
    annuli, comps, _ = start_basis.shape
    chunk, frames, parts = pixels // nfrm, width * nfrm, npix * nfrm
    rows = comps * frames // LANES // parts
    narrow = jnp.bfloat16 if rows % 16 == 0 else jnp.float32

    smem = pl.BlockSpec(memory_space=pltpu.SMEM)
    vmem = pl.BlockSpec(memory_space=pltpu.VMEM)
    hbm = pl.BlockSpec(memory_space=pltpu.HBM)
    shape = jax.ShapeDtypeStruct

    def call(kernel, out, ins, outs, name, scratch=(), mib=32):
        return pl.pallas_call(
            kernel,
            out_shape=out,
            in_specs=ins,
            out_specs=outs,
            scratch_shapes=list(scratch),
            compiler_params=pltpu.CompilerParams(vmem_limit_bytes=mib * 1024 * 1024),
            name=name,
        )

    def rotate(x, shift):
        return lax.ppermute(x, "frm", [(i, (i + shift) % nfrm) for i in range(nfrm)])

    starts = [rotate(start_basis, shift) for shift in range(1, nfrm)]
    messages = call(
        pack_kernel,
        [shape((chunk, width), jnp.bfloat16)] * (nfrm - 1),
        [hbm],
        [vmem] * (nfrm - 1),
        "pack",
        [pltpu.SemaphoreType.DMA((nfrm - 1,))],
    )(curves)
    got = [rotate(message, shift) for shift, message in enumerate(messages, 1)]
    own, raw, weight, say, marks = call(
        functools.partial(own_kernel, block, parts // (npix * nblocks)),
        (
            shape((chunk, width), jnp.bfloat16),
            shape((comps, chunk), jnp.float32),
            shape((1, chunk), jnp.float32),
            shape((1, LANES), jnp.float32),
            shape((parts, LANES), jnp.int32),
        ),
        [smem, smem, vmem, hbm, hbm],
        (vmem, vmem, vmem, vmem, vmem),
        "own_part",
        [
            pltpu.VMEM((comps, width), jnp.bfloat16),
            pltpu.SMEM((npix * nblocks,), jnp.int32),
            pltpu.SemaphoreType.DMA((2,)),
        ],
    )(annulus_of_block, ref_blocks, keep_mask.reshape(nfrm, chunk), curves, start_basis)
    held = [own, *got]
    sent = call(
        functools.partial(first_kernel, block, nfrm),
        shape((parts, rows, LANES), jnp.float32),
        [smem] + [vmem] * (4 + 2 * (nfrm - 1)),
        vmem,
        "first_span",
    )(annulus_of_block, raw, weight, say, own, *got, *starts)

    give = None
    for step in range(ITERS):
        kind = narrow if step else jnp.float32
        taken = lax.all_to_all(sent, BOTH, 0, 0, tiled=True)
        total = shape((parts, rows, LANES), kind)
        if step == 0:
            total, give = call(
                functools.partial(first_sum_kernel, annuli),
                (total, shape((parts, LANES), jnp.int32)),
                [vmem, vmem],
                (vmem, vmem),
                "first_sum",
            )(taken, marks)
        else:
            total = call(
                functools.partial(sum_kernel, annuli), total, [vmem, vmem], vmem, "sum"
            )(taken, give)
        span = lax.all_to_all(total, BOTH, 0, 0, tiled=True)
        last = step == ITERS - 1
        sent = call(
            functools.partial(step_kernel, last, nfrm),
            shape((comps, chunk), jnp.float32) if last else shape((parts, rows, LANES), narrow),
            [vmem] * (2 + nfrm),
            vmem,
            "fit" if last else "step",
            [pltpu.VMEM((comps, frames), kind)],
        )(span, weight, *held)

    if nfrm == 2 and chunk == block:
        return call(
            place_kernel,
            shape((nblocks, comps, chunk), jnp.float32),
            [vmem, vmem],
            hbm,
            "place",
            [pltpu.SemaphoreType.DMA((2,))],
        )(sent, rotate(sent, 1))
    every = lax.all_gather(sent, "frm")
    return every.swapaxes(0, 1).reshape(comps, nblocks, block).swapaxes(0, 1)


def solution(mesh):
    in_specs = (P("pix", "frm"), P("pix"), P(), P("pix", None), P(None, None, "frm"))
    out_specs = P("pix", None, None)
    body = functools.partial(shards, mesh.shape["pix"], mesh.shape["frm"])
    return jax.shard_map(body, mesh=mesh, in_specs=in_specs, out_specs=out_specs, check_vma=False)
```

```python
import functools

import jax
import jax.numpy as jnp
from jax import lax
from jax.experimental import pallas as pl
from jax.experimental.pallas import tpu as pltpu
from jax.sharding import PartitionSpec as P

ITERS = 4
LANES = 128
PANEL = 16
BOTH = ("pix", "frm")
EXACT = lax.Precision.HIGHEST
ROWS_TO_ROWS = (((1,), (1,)), ((), ()))


def solve_rows(gram, raw):
    k = gram.shape[0]
    rows = lax.broadcasted_iota(jnp.int32, (k, LANES), 0)
    low = jnp.concatenate([gram, jnp.zeros((k, LANES - k), jnp.float32)], axis=1)
    wide = raw.shape[1] // LANES if raw.shape[1] % LANES == 0 else 1
    size = raw.shape[1] // wide
    right = [raw[:, t * size : (t + 1) * size] for t in range(wide)]
    done = [[] for _ in right]
    pivots = jnp.zeros((k, LANES), jnp.float32)
    for base in range(0, k, PANEL):
        below = rows[base:, :]
        panel = [jnp.broadcast_to(low[:, base + j : base + j + 1], low.shape) for j in range(PANEL)]
        pivot = panel[0][:1, :]
        for j in range(PANEL):
            inverse = 1.0 / pivot
            pivots = jnp.where(rows == base + j, pivot, pivots)
            if j + 1 < PANEL:
                beside = panel[j + 1][j : j + 1, :]
                pivot = panel[j + 1][j + 1 : j + 2, :] - beside * beside * inverse
            factor = jnp.where(below > base + j, panel[j] * inverse, 0.0)
            for i in range(j + 1, PANEL):
                panel[i] = panel[i] - factor * panel[i][j : j + 1, :]
            if base + PANEL < k:
                low = low - factor * low[j : j + 1, :]
            right = [x - factor[:, :size] * x[j : j + 1, :] for x in right]
        low = low[PANEL:, :]
        for held, x in zip(done, right):
            held.append(x[:PANEL, :])
        right = [x[PANEL:, :] for x in right]
    scale = lax.rsqrt(pivots)[:, :size]
    return jnp.concatenate([jnp.concatenate(held, axis=0) * scale for held in done], axis=1)


def pieces(wide):
    high = wide.astype(jnp.bfloat16)
    rest = wide - high.astype(jnp.float32)
    middle = rest.astype(jnp.bfloat16)
    low = (rest - middle.astype(jnp.float32)).astype(jnp.bfloat16)
    return jnp.concatenate([high, middle, low], axis=0)


def fold(stacked, k):
    return (stacked[2 * k :] + stacked[k : 2 * k]) + stacked[:k]


def dot_rows(left, right):
    return lax.dot_general(left, right, ROWS_TO_ROWS, preferred_element_type=jnp.float32)


def store_tiles(span, first, across, out_ref):
    rows = out_ref.shape[1]
    for down in range(span.shape[0] // rows):
        for along in range(span.shape[1] // LANES):
            tile = span[down * rows : (down + 1) * rows, along * LANES : (along + 1) * LANES]
            out_ref[first + (down * across + along)] = tile.astype(out_ref.dtype)


def span_of(proj, weight, held, sources, out_ref):
    proj_bf = (proj * weight).astype(jnp.bfloat16)
    width = held[0].shape[1] // LANES
    for curves, source in zip(held, sources):
        span = jnp.dot(proj_bf, curves[...], preferred_element_type=jnp.float32)
        yield span, source * width, width * len(held)


def frame_order(others):
    frm = lax.axis_index("frm")
    return [lax.rem(frm - shift + others, others) for shift in range(others)]


def pack_kernel(own_ref, *refs):
    out_refs, sems = refs[:-1], refs[-1]
    others = len(out_refs) + 1
    chunk = out_refs[0].shape[0]
    copies = []
    for shift, out_ref in enumerate(out_refs, 1):
        target = lax.rem(lax.axis_index("frm") + shift, others)
        rows = pl.ds(pl.multiple_of(target * chunk, chunk), chunk)
        copies.append(pltpu.make_async_copy(own_ref.at[rows], out_ref, sems.at[shift - 1]))
    for copy in copies:
        copy.start()
    for copy in copies:
        copy.wait()


def own_kernel(
    block, chunks, ann_ref, listed_ref, keep_ref, all_ref, start_ref,
    own_ref, raw_ref, weight_ref, say_ref, mark_ref, basis, table, sems,
):
    pix, frm = lax.axis_index("pix"), lax.axis_index("frm")
    chunk = own_ref.shape[0]
    rows = pl.ds(pl.multiple_of(frm * chunk, chunk), chunk)
    place = frm * chunk // block
    label = ann_ref[place]
    curves = pltpu.make_async_copy(all_ref.at[rows], own_ref, sems.at[0])
    start = pltpu.make_async_copy(start_ref.at[label], basis, sems.at[1])
    curves.start()
    start.start()
    for b in range(table.shape[0]):
        table[b] = -1
    for a in range(listed_ref.shape[0]):
        for entry in range(listed_ref.shape[1]):
            table[listed_ref[a, entry]] = a
    for j in range(mark_ref.shape[0]):
        mark_ref[j : j + 1, :] = jnp.full((1, LANES), table[j // chunks], jnp.int32)
    listed = (table[pix * ann_ref.shape[0] + place] >= 0).astype(jnp.int32)
    kept = keep_ref[pl.ds(frm, 1), :]
    weight_ref[...] = jnp.where(kept == 1, listed, 0).astype(jnp.float32)
    say_ref[...] = jnp.full((1, LANES), (1 - listed) * label, jnp.int32).astype(jnp.float32)
    curves.wait()
    start.wait()
    raw_ref[...] = dot_rows(basis[...], own_ref[...])


def first_kernel(block, others, ann_ref, raw_ref, weight_ref, say_ref, own_ref, *refs):
    got, starts, out_ref = refs[: others - 1], refs[others - 1 : -1], refs[-1]
    label = ann_ref[lax.axis_index("frm") * own_ref.shape[0] // block]
    proj = raw_ref[...]
    for curves, start in zip(got, starts):
        proj = proj + dot_rows(start[label], curves[...])
    held, weight = (own_ref, *got), weight_ref[...]
    for span, first, across in span_of(proj, weight, held, frame_order(others), out_ref):
        store_tiles(
            jnp.concatenate(
                [
                    span[:, i : i + LANES] + say_ref[...]
                    for i in range(0, span.shape[1], LANES)
                ],
                axis=1,
            ),
            first,
            across,
            out_ref,
        )


def step_kernel(last, others, span_ref, weight_ref, *refs):
    held, (out_ref, whole) = refs[:others], refs[others:]
    parts, rows = span_ref.shape[:2]
    comps, frames = whole.shape
    across, width = frames // LANES, frames // others
    for j in range(parts):
        down, along = j // across * rows, j % across * LANES
        whole[down : down + rows, along : along + LANES] = span_ref[j]
    span, sources = whole[...], frame_order(others)
    raw = jnp.zeros((comps, held[0].shape[0]), jnp.float32)
    for curves, source in zip(held, sources):
        part = whole[:, pl.ds(pl.multiple_of(source * width, LANES), width)]
        if span.dtype == jnp.bfloat16:
            raw = raw + dot_rows(part, curves[...])
        else:
            raw = raw + fold(dot_rows(pieces(part), curves[...]), comps)
    if span.dtype == jnp.bfloat16:
        gram = dot_rows(span, span)
    else:
        gram = lax.dot_general(
            span, span, ROWS_TO_ROWS, precision=EXACT, preferred_element_type=jnp.float32
        )
    proj = solve_rows(gram, raw)
    if last:
        out_ref[...] = proj
    else:
        for span, first, across in span_of(proj, weight_ref[...], held, sources, out_ref):
            store_tiles(span, first, across, out_ref)


def place_kernel(own_ref, other_ref, out_ref, sems):
    frm = lax.axis_index("frm")
    copies = [
        pltpu.make_async_copy(own_ref, out_ref.at[frm], sems.at[0]),
        pltpu.make_async_copy(other_ref, out_ref.at[1 - frm], sems.at[1]),
    ]
    for copy in copies:
        copy.start()
    for copy in copies:
        copy.wait()


def add_and_give(annuli, in_ref, mark_ref, give_ref, out_ref):
    parts, rows = out_ref.shape[:2]

    def add(j, sums):
        part = in_ref[j].astype(jnp.float32)
        mark = mark_ref[pl.ds(j, 1), :]
        return tuple(s + jnp.where(mark == a, part, 0.0) for a, s in enumerate(sums))

    def give(j, sums):
        mark = give_ref[pl.ds(j, 1), :]
        total = sums[0]
        for a in range(1, annuli):
            total = jnp.where(mark == a, sums[a], total)
        out_ref[j] = total.astype(out_ref.dtype)
        return sums

    sums = tuple(jnp.zeros((rows, LANES), jnp.float32) for _ in range(annuli))
    if parts <= 32:
        for j in range(parts):
            sums = add(j, sums)
        for j in range(parts):
            give(j, sums)
    else:
        sums = lax.fori_loop(0, parts, add, sums)
        lax.fori_loop(0, parts, give, sums)


def first_sum_kernel(annuli, in_ref, mark_ref, out_ref, give_ref):
    for j in range(in_ref.shape[0]):
        label = mark_ref[j : j + 1, :]
        said = in_ref[j, :1, :].astype(jnp.int32)
        give_ref[j : j + 1, :] = jnp.where(label < 0, said, label)
    add_and_give(annuli, in_ref, mark_ref, give_ref, out_ref)


def sum_kernel(annuli, in_ref, give_ref, out_ref):
    add_and_give(annuli, in_ref, give_ref, give_ref, out_ref)


def shards(npix, nfrm, curves, annulus_of_block, ref_blocks, keep_mask, start_basis):
    pixels, width = curves.shape
    nblocks, block = keep_mask.shape
    annuli, comps, _ = start_basis.shape
    chunk, frames, parts = pixels // nfrm, width * nfrm, npix * nfrm
    rows = comps * frames // LANES // parts
    narrow = jnp.bfloat16 if rows % 16 == 0 else jnp.float32

    smem = pl.BlockSpec(memory_space=pltpu.SMEM)
    vmem = pl.BlockSpec(memory_space=pltpu.VMEM)
    hbm = pl.BlockSpec(memory_space=pltpu.HBM)
    shape = jax.ShapeDtypeStruct

    def call(kernel, out, ins, outs, name, scratch=(), mib=32):
        return pl.pallas_call(
            kernel,
            out_shape=out,
            in_specs=ins,
            out_specs=outs,
            scratch_shapes=list(scratch),
            compiler_params=pltpu.CompilerParams(vmem_limit_bytes=mib * 1024 * 1024),
            name=name,
        )

    def rotate(x, shift):
        return lax.ppermute(x, "frm", [(i, (i + shift) % nfrm) for i in range(nfrm)])

    starts = [rotate(start_basis, shift) for shift in range(1, nfrm)]
    messages = call(
        pack_kernel,
        [shape((chunk, width), jnp.bfloat16)] * (nfrm - 1),
        [hbm],
        [vmem] * (nfrm - 1),
        "pack",
        [pltpu.SemaphoreType.DMA((nfrm - 1,))],
    )(curves)
    got = [rotate(message, shift) for shift, message in enumerate(messages, 1)]
    own, raw, weight, say, marks = call(
        functools.partial(own_kernel, block, parts // (npix * nblocks)),
        (
            shape((chunk, width), jnp.bfloat16),
            shape((comps, chunk), jnp.float32),
            shape((1, chunk), jnp.float32),
            shape((1, LANES), jnp.float32),
            shape((parts, LANES), jnp.int32),
        ),
        [smem, smem, vmem, hbm, hbm],
        (vmem, vmem, vmem, vmem, vmem),
        "own_part",
        [
            pltpu.VMEM((comps, width), jnp.bfloat16),
            pltpu.SMEM((npix * nblocks,), jnp.int32),
            pltpu.SemaphoreType.DMA((2,)),
        ],
    )(annulus_of_block, ref_blocks, keep_mask.reshape(nfrm, chunk), curves, start_basis)
    held = [own, *got]
    sent = call(
        functools.partial(first_kernel, block, nfrm),
        shape((parts, rows, LANES), jnp.float32),
        [smem] + [vmem] * (4 + 2 * (nfrm - 1)),
        vmem,
        "first_span",
    )(annulus_of_block, raw, weight, say, own, *got, *starts)

    give = None
    for step in range(ITERS):
        kind = narrow if step else jnp.float32
        taken = lax.all_to_all(sent, BOTH, 0, 0, tiled=True)
        total = shape((parts, rows, LANES), kind)
        if step == 0:
            total, give = call(
                functools.partial(first_sum_kernel, annuli),
                (total, shape((parts, LANES), jnp.int32)),
                [vmem, vmem],
                (vmem, vmem),
                "first_sum",
            )(taken, marks)
        else:
            total = call(
                functools.partial(sum_kernel, annuli), total, [vmem, vmem], vmem, "sum"
            )(taken, give)
        span = lax.all_to_all(total, BOTH, 0, 0, tiled=True)
        last = step == ITERS - 1
        sent = call(
            functools.partial(step_kernel, last, nfrm),
            shape((comps, chunk), jnp.float32) if last else shape((parts, rows, LANES), narrow),
            [vmem] * (2 + nfrm),
            vmem,
            "fit" if last else "step",
            [pltpu.VMEM((comps, frames), kind)],
        )(span, weight, *held)

    if nfrm == 2 and chunk == block:
        return call(
            place_kernel,
            shape((nblocks, comps, chunk), jnp.float32),
            [vmem, vmem],
            hbm,
            "place",
            [pltpu.SemaphoreType.DMA((2,))],
        )(sent, rotate(sent, 1))
    every = lax.all_gather(sent, "frm")
    return every.swapaxes(0, 1).reshape(comps, nblocks, block).swapaxes(0, 1)


def solution(mesh):
    in_specs = (P("pix", "frm"), P("pix"), P(), P("pix", None), P(None, None, "frm"))
    out_specs = P("pix", None, None)
    body = functools.partial(shards, mesh.shape["pix"], mesh.shape["frm"])
    return jax.shard_map(body, mesh=mesh, in_specs=in_specs, out_specs=out_specs, check_vma=False)
```

```python
import functools

import jax
import jax.numpy as jnp
from jax import lax
from jax.experimental import pallas as pl
from jax.experimental.pallas import tpu as pltpu
from jax.sharding import PartitionSpec as P

ITERS = 4
LANES = 128
PANEL = 16
BOTH = ("pix", "frm")
EXACT = lax.Precision.HIGHEST
ROWS_TO_ROWS = (((1,), (1,)), ((), ()))


def solve_rows(gram, raw):
    k = gram.shape[0]
    rows = lax.broadcasted_iota(jnp.int32, (k, LANES), 0)
    low = jnp.concatenate([gram, jnp.zeros((k, LANES - k), jnp.float32)], axis=1)
    wide = raw.shape[1] // LANES if raw.shape[1] % LANES == 0 else 1
    size = raw.shape[1] // wide
    right = [raw[:, t * size : (t + 1) * size] for t in range(wide)]
    done = [[] for _ in right]
    pivots = jnp.zeros((k, LANES), jnp.float32)
    for base in range(0, k, PANEL):
        below = rows[base:, :]
        panel = [jnp.broadcast_to(low[:, base + j : base + j + 1], low.shape) for j in range(PANEL)]
        pivot = panel[0][:1, :]
        for j in range(PANEL):
            inverse = 1.0 / pivot
            pivots = jnp.where(rows == base + j, pivot, pivots)
            if j + 1 < PANEL:
                beside = panel[j + 1][j : j + 1, :]
                pivot = panel[j + 1][j + 1 : j + 2, :] - beside * beside * inverse
            factor = jnp.where(below > base + j, panel[j] * inverse, 0.0)
            for i in range(j + 1, PANEL):
                panel[i] = panel[i] - factor * panel[i][j : j + 1, :]
            if base + PANEL < k:
                low = low - factor * low[j : j + 1, :]
            right = [x - factor[:, :size] * x[j : j + 1, :] for x in right]
        low = low[PANEL:, :]
        for held, x in zip(done, right):
            held.append(x[:PANEL, :])
        right = [x[PANEL:, :] for x in right]
    scale = lax.rsqrt(pivots)[:, :size]
    return jnp.concatenate([jnp.concatenate(held, axis=0) * scale for held in done], axis=1)


def pieces(wide):
    high = wide.astype(jnp.bfloat16)
    rest = wide - high.astype(jnp.float32)
    middle = rest.astype(jnp.bfloat16)
    low = (rest - middle.astype(jnp.float32)).astype(jnp.bfloat16)
    return jnp.concatenate([high, middle, low], axis=0)


def fold(stacked, k):
    return (stacked[2 * k :] + stacked[k : 2 * k]) + stacked[:k]


def dot_rows(left, right):
    return lax.dot_general(left, right, ROWS_TO_ROWS, preferred_element_type=jnp.float32)


def store_tiles(span, first, across, out_ref):
    rows = out_ref.shape[1]
    for down in range(span.shape[0] // rows):
        for along in range(span.shape[1] // LANES):
            tile = span[down * rows : (down + 1) * rows, along * LANES : (along + 1) * LANES]
            out_ref[first + (down * across + along)] = tile.astype(out_ref.dtype)


def mine(curves, chunk):
    if curves.shape[0] == chunk:
        return curves[...]
    return curves[pl.ds(pl.multiple_of(lax.axis_index("frm") * chunk, chunk), chunk), :]


def span_of(proj, weight, held, sources, out_ref):
    proj_bf = (proj * weight).astype(jnp.bfloat16)
    width = held[0].shape[1] // LANES
    for curves, source in zip(held, sources):
        span = jnp.dot(proj_bf, mine(curves, proj.shape[1]), preferred_element_type=jnp.float32)
        yield span, source * width, width * len(held)


def frame_order(others):
    frm = lax.axis_index("frm")
    return [lax.rem(frm - shift + others, others) for shift in range(others)]


def pack_kernel(own_ref, *refs):
    out_refs, sems = refs[:-1], refs[-1]
    others = len(out_refs) + 1
    chunk = out_refs[0].shape[0]
    copies = []
    for shift, out_ref in enumerate(out_refs, 1):
        target = lax.rem(lax.axis_index("frm") + shift, others)
        rows = pl.ds(pl.multiple_of(target * chunk, chunk), chunk)
        copies.append(pltpu.make_async_copy(own_ref.at[rows], out_ref, sems.at[shift - 1]))
    for copy in copies:
        copy.start()
    for copy in copies:
        copy.wait()


def entry(row_ref, at):
    lanes = lax.broadcasted_iota(jnp.int32, row_ref.shape, 1)
    return jnp.sum(jnp.where(lanes == at, row_ref[...], 0).astype(jnp.float32)).astype(jnp.int32)


def pick_kernel(block, chunk, ann_ref, start_ref, *out_refs):
    others = len(out_refs) + 1
    for shift, out_ref in enumerate(out_refs, 1):
        target = lax.rem(lax.axis_index("frm") + shift, others)
        out_ref[...] = start_ref[entry(ann_ref, target * chunk // block)]


def own_kernel(
    block, others, chunks, ann_ref, listed_ref, keep_ref, own_ref, start_ref,
    raw_ref, weight_ref, say_ref, mark_ref,
):
    pix, frm = lax.axis_index("pix"), lax.axis_index("frm")
    chunk = raw_ref.shape[1]
    label = entry(ann_ref, frm * chunk // block)
    raw_ref[...] = dot_rows(start_ref[label], mine(own_ref, chunk))
    blocks = lax.broadcasted_iota(jnp.int32, mark_ref.shape, 0) // chunks
    marks = jnp.full(mark_ref.shape, -1, jnp.int32)
    for a in range(listed_ref.shape[0]):
        for at in range(listed_ref.shape[1]):
            marks = jnp.where(blocks == listed_ref[a : a + 1, at : at + 1], a, marks)
    mark_ref[...] = marks
    listed = mark_ref[pl.ds(pix * others + frm, 1), :] >= 0
    kept = keep_ref[pl.ds(frm, 1), :]
    weight_ref[...] = jnp.where((kept == 1) & listed[:, :1], 1.0, 0.0)
    say_ref[...] = jnp.where(listed, 0, label).astype(jnp.float32)


def first_kernel(others, raw_ref, weight_ref, say_ref, own_ref, *refs):
    got, starts, out_ref = refs[: others - 1], refs[others - 1 : -1], refs[-1]
    proj = raw_ref[...]
    for curves, start in zip(got, starts):
        proj = proj + dot_rows(start[...], curves[...])
    held, weight = (own_ref, *got), weight_ref[...]
    for span, first, across in span_of(proj, weight, held, frame_order(others), out_ref):
        store_tiles(
            jnp.concatenate(
                [
                    span[:, i : i + LANES] + say_ref[...]
                    for i in range(0, span.shape[1], LANES)
                ],
                axis=1,
            ),
            first,
            across,
            out_ref,
        )


def step_kernel(last, others, span_ref, weight_ref, *refs):
    held, (out_ref, whole) = refs[:others], refs[others:]
    parts, rows = span_ref.shape[:2]
    comps, frames = whole.shape
    across, width = frames // LANES, frames // others
    for j in range(parts):
        down, along = j // across * rows, j % across * LANES
        whole[down : down + rows, along : along + LANES] = span_ref[j]
    span, sources = whole[...], frame_order(others)
    chunk = weight_ref.shape[1]
    raw = jnp.zeros((comps, chunk), jnp.float32)
    for curves, source in zip(held, sources):
        part = whole[:, pl.ds(pl.multiple_of(source * width, LANES), width)]
        if span.dtype == jnp.bfloat16:
            raw = raw + dot_rows(part, mine(curves, chunk))
        else:
            raw = raw + fold(dot_rows(pieces(part), mine(curves, chunk)), comps)
    if span.dtype == jnp.bfloat16:
        gram = dot_rows(span, span)
    else:
        gram = lax.dot_general(
            span, span, ROWS_TO_ROWS, precision=EXACT, preferred_element_type=jnp.float32
        )
    proj = solve_rows(gram, raw)
    if last:
        out_ref[...] = proj
    else:
        for span, first, across in span_of(proj, weight_ref[...], held, sources, out_ref):
            store_tiles(span, first, across, out_ref)


def place_kernel(own_ref, other_ref, out_ref, sems):
    frm = lax.axis_index("frm")
    copies = [
        pltpu.make_async_copy(own_ref, out_ref.at[frm], sems.at[0]),
        pltpu.make_async_copy(other_ref, out_ref.at[1 - frm], sems.at[1]),
    ]
    for copy in copies:
        copy.start()
    for copy in copies:
        copy.wait()


def add_and_give(annuli, in_ref, mark_ref, give_ref, out_ref):
    parts, rows = out_ref.shape[:2]

    def add(j, sums):
        part = in_ref[j].astype(jnp.float32)
        mark = mark_ref[pl.ds(j, 1), :]
        return tuple(s + jnp.where(mark == a, part, 0.0) for a, s in enumerate(sums))

    def give(j, sums):
        mark = give_ref[pl.ds(j, 1), :]
        total = sums[0]
        for a in range(1, annuli):
            total = jnp.where(mark == a, sums[a], total)
        out_ref[j] = total.astype(out_ref.dtype)
        return sums

    sums = tuple(jnp.zeros((rows, LANES), jnp.float32) for _ in range(annuli))
    if parts <= 32:
        for j in range(parts):
            sums = add(j, sums)
        for j in range(parts):
            give(j, sums)
    else:
        sums = lax.fori_loop(0, parts, add, sums)
        lax.fori_loop(0, parts, give, sums)


def first_sum_kernel(annuli, in_ref, mark_ref, out_ref, give_ref):
    for j in range(in_ref.shape[0]):
        label = mark_ref[j : j + 1, :]
        said = in_ref[j, :1, :].astype(jnp.int32)
        give_ref[j : j + 1, :] = jnp.where(label < 0, said, label)
    add_and_give(annuli, in_ref, mark_ref, give_ref, out_ref)


def sum_kernel(annuli, in_ref, give_ref, out_ref):
    add_and_give(annuli, in_ref, give_ref, give_ref, out_ref)


def shards(npix, nfrm, curves, annulus_of_block, ref_blocks, keep_mask, start_basis):
    pixels, width = curves.shape
    nblocks, block = keep_mask.shape
    annuli, comps, _ = start_basis.shape
    chunk, frames, parts = pixels // nfrm, width * nfrm, npix * nfrm
    rows = comps * frames // LANES // parts
    narrow = jnp.bfloat16 if rows % 16 == 0 else jnp.float32

    labels = annulus_of_block.reshape(1, nblocks)
    vmem = pl.BlockSpec(memory_space=pltpu.VMEM)
    hbm = pl.BlockSpec(memory_space=pltpu.HBM)
    shape = jax.ShapeDtypeStruct

    def call(kernel, out, ins, outs, name, scratch=(), mib=32):
        return pl.pallas_call(
            kernel,
            out_shape=out,
            in_specs=ins,
            out_specs=outs,
            scratch_shapes=list(scratch),
            compiler_params=pltpu.CompilerParams(vmem_limit_bytes=mib * 1024 * 1024),
            name=name,
        )

    def rotate(x, shift):
        return lax.ppermute(x, "frm", [(i, (i + shift) % nfrm) for i in range(nfrm)])

    messages = call(
        pack_kernel,
        [shape((chunk, width), jnp.bfloat16)] * (nfrm - 1),
        [hbm],
        [vmem] * (nfrm - 1),
        "pack",
        [pltpu.SemaphoreType.DMA((nfrm - 1,))],
    )(curves)
    got = [rotate(message, shift) for shift, message in enumerate(messages, 1)]
    picks = call(
        functools.partial(pick_kernel, block, chunk),
        [shape((comps, width), jnp.bfloat16)] * (nfrm - 1),
        [vmem, vmem],
        [vmem] * (nfrm - 1),
        "pick",
    )(labels, start_basis)
    starts = [rotate(pick, shift) for shift, pick in enumerate(picks, 1)]
    raw, weight, say, marks = call(
        functools.partial(own_kernel, block, nfrm, parts // (npix * nblocks)),
        (
            shape((comps, chunk), jnp.float32),
            shape((1, chunk), jnp.float32),
            shape((1, LANES), jnp.float32),
            shape((parts, LANES), jnp.int32),
        ),
        [vmem] * 5,
        (vmem, vmem, vmem, vmem),
        "own_part",
    )(labels, ref_blocks, keep_mask.reshape(nfrm, chunk), curves, start_basis)
    held = [curves, *got]
    sent = call(
        functools.partial(first_kernel, nfrm),
        shape((parts, rows, LANES), jnp.float32),
        [vmem] * (4 + 2 * (nfrm - 1)),
        vmem,
        "first_span",
    )(raw, weight, say, curves, *got, *starts)

    give = None
    for step in range(ITERS):
        kind = narrow if step else jnp.float32
        taken = lax.all_to_all(sent, BOTH, 0, 0, tiled=True)
        total = shape((parts, rows, LANES), kind)
        if step == 0:
            total, give = call(
                functools.partial(first_sum_kernel, annuli),
                (total, shape((parts, LANES), jnp.int32)),
                [vmem, vmem],
                (vmem, vmem),
                "first_sum",
            )(taken, marks)
        else:
            total = call(
                functools.partial(sum_kernel, annuli), total, [vmem, vmem], vmem, "sum"
            )(taken, give)
        span = lax.all_to_all(total, BOTH, 0, 0, tiled=True)
        last = step == ITERS - 1
        sent = call(
            functools.partial(step_kernel, last, nfrm),
            shape((comps, chunk), jnp.float32) if last else shape((parts, rows, LANES), narrow),
            [vmem] * (2 + nfrm),
            vmem,
            "fit" if last else "step",
            [pltpu.VMEM((comps, frames), kind)],
        )(span, weight, *held)

    if nfrm == 2 and chunk == block:
        return call(
            place_kernel,
            shape((nblocks, comps, chunk), jnp.float32),
            [vmem, vmem],
            hbm,
            "place",
            [pltpu.SemaphoreType.DMA((2,))],
        )(sent, rotate(sent, 1))
    every = lax.all_gather(sent, "frm")
    return every.swapaxes(0, 1).reshape(comps, nblocks, block).swapaxes(0, 1)


def solution(mesh):
    in_specs = (P("pix", "frm"), P("pix"), P(), P("pix", None), P(None, None, "frm"))
    out_specs = P("pix", None, None)
    body = functools.partial(shards, mesh.shape["pix"], mesh.shape["frm"])
    return jax.shard_map(body, mesh=mesh, in_specs=in_specs, out_specs=out_specs, check_vma=False)
```

```python
import functools

import jax
import jax.numpy as jnp
from jax import lax
from jax.experimental import pallas as pl
from jax.experimental.pallas import tpu as pltpu
from jax.sharding import PartitionSpec as P

ITERS = 4
LANES = 128
PANEL = 16
BOTH = ("frm", "pix")
EXACT = lax.Precision.HIGHEST
ROWS_TO_ROWS = (((1,), (1,)), ((), ()))


def solve_rows(gram, raw):
    k = gram.shape[0]
    rows = lax.broadcasted_iota(jnp.int32, (k, LANES), 0)
    low = jnp.concatenate([gram, jnp.zeros((k, LANES - k), jnp.float32)], axis=1)
    wide = raw.shape[1] // LANES if raw.shape[1] % LANES == 0 else 1
    size = raw.shape[1] // wide
    right = [raw[:, t * size : (t + 1) * size] for t in range(wide)]
    done = [[] for _ in right]
    pivots = jnp.zeros((k, LANES), jnp.float32)
    for base in range(0, k, PANEL):
        below = rows[base:, :]
        panel = [jnp.broadcast_to(low[:, base + j : base + j + 1], low.shape) for j in range(PANEL)]
        pivot = panel[0][:1, :]
        for j in range(PANEL):
            inverse = 1.0 / pivot
            pivots = jnp.where(rows == base + j, pivot, pivots)
            if j + 1 < PANEL:
                beside = panel[j + 1][j : j + 1, :]
                pivot = panel[j + 1][j + 1 : j + 2, :] - beside * beside * inverse
            factor = jnp.where(below > base + j, panel[j] * inverse, 0.0)
            for i in range(j + 1, PANEL):
                panel[i] = panel[i] - factor * panel[i][j : j + 1, :]
            if base + PANEL < k:
                low = low - factor * low[j : j + 1, :]
            right = [x - factor[:, :size] * x[j : j + 1, :] for x in right]
        low = low[PANEL:, :]
        for held, x in zip(done, right):
            held.append(x[:PANEL, :])
        right = [x[PANEL:, :] for x in right]
    scale = lax.rsqrt(pivots)[:, :size]
    return jnp.concatenate([jnp.concatenate(held, axis=0) * scale for held in done], axis=1)


def pieces(wide):
    high = wide.astype(jnp.bfloat16)
    rest = wide - high.astype(jnp.float32)
    middle = rest.astype(jnp.bfloat16)
    low = (rest - middle.astype(jnp.float32)).astype(jnp.bfloat16)
    return jnp.concatenate([high, middle, low], axis=0)


def fold(stacked, k):
    return (stacked[2 * k :] + stacked[k : 2 * k]) + stacked[:k]


def dot_rows(left, right):
    return lax.dot_general(left, right, ROWS_TO_ROWS, preferred_element_type=jnp.float32)


def store_tiles(span, first, across, out_ref):
    rows = out_ref.shape[1]
    for down in range(span.shape[0] // rows):
        for along in range(span.shape[1] // LANES):
            tile = span[down * rows : (down + 1) * rows, along * LANES : (along + 1) * LANES]
            out_ref[first + (down * across + along)] = tile.astype(out_ref.dtype)


def mine(curves, chunk):
    if curves.shape[0] == chunk:
        return curves[...]
    return curves[pl.ds(pl.multiple_of(lax.axis_index("frm") * chunk, chunk), chunk), :]


def span_of(proj, weight, held, sources, out_ref):
    proj_bf = (proj * weight).astype(jnp.bfloat16)
    width = held[0].shape[1] // LANES
    for curves, source in zip(held, sources):
        span = jnp.dot(proj_bf, mine(curves, proj.shape[1]), preferred_element_type=jnp.float32)
        yield span, source * width, width * len(held)


def frame_order(others):
    frm = lax.axis_index("frm")
    return [lax.rem(frm - shift + others, others) for shift in range(others)]


def pack_kernel(own_ref, *refs):
    out_refs, sems = refs[:-1], refs[-1]
    others = len(out_refs) + 1
    chunk = out_refs[0].shape[0]
    copies = []
    for shift, out_ref in enumerate(out_refs, 1):
        target = lax.rem(lax.axis_index("frm") + shift, others)
        rows = pl.ds(pl.multiple_of(target * chunk, chunk), chunk)
        copies.append(pltpu.make_async_copy(own_ref.at[rows], out_ref, sems.at[shift - 1]))
    for copy in copies:
        copy.start()
    for copy in copies:
        copy.wait()


def entry(row_ref, at):
    lanes = lax.broadcasted_iota(jnp.int32, row_ref.shape, 1)
    return jnp.sum(jnp.where(lanes == at, row_ref[...], 0).astype(jnp.float32)).astype(jnp.int32)


def pick_kernel(block, chunk, ann_ref, start_ref, *out_refs):
    others = len(out_refs) + 1
    for shift, out_ref in enumerate(out_refs, 1):
        target = lax.rem(lax.axis_index("frm") + shift, others)
        out_ref[...] = start_ref[entry(ann_ref, target * chunk // block)]


def own_kernel(
    block, others, ann_ref, listed_ref, keep_ref, own_ref, start_ref,
    raw_ref, weight_ref, say_ref, mark_ref,
):
    pix, frm = lax.axis_index("pix"), lax.axis_index("frm")
    chunk = raw_ref.shape[1]
    label = entry(ann_ref, frm * chunk // block)
    raw_ref[...] = dot_rows(start_ref[label], mine(own_ref, chunk))
    npix = mark_ref.shape[0] // others
    place = lax.broadcasted_iota(jnp.int32, mark_ref.shape, 0)
    blocks = place % npix * ann_ref.shape[1] + place // npix * chunk // block
    marks = jnp.full(mark_ref.shape, -1, jnp.int32)
    for a in range(listed_ref.shape[0]):
        for at in range(listed_ref.shape[1]):
            marks = jnp.where(blocks == listed_ref[a : a + 1, at : at + 1], a, marks)
    mark_ref[...] = marks
    listed = mark_ref[pl.ds(frm * npix + pix, 1), :] >= 0
    kept = keep_ref[pl.ds(frm, 1), :]
    weight_ref[...] = jnp.where((kept == 1) & listed[:, :1], 1.0, 0.0)
    say_ref[...] = jnp.where(listed, 0, label).astype(jnp.float32)


def first_kernel(others, raw_ref, weight_ref, say_ref, own_ref, *refs):
    got, starts, out_ref = refs[: others - 1], refs[others - 1 : -1], refs[-1]
    proj = raw_ref[...]
    for curves, start in zip(got, starts):
        proj = proj + dot_rows(start[...], curves[...])
    held, weight = (own_ref, *got), weight_ref[...]
    for span, first, across in span_of(proj, weight, held, frame_order(others), out_ref):
        store_tiles(
            jnp.concatenate(
                [
                    span[:, i : i + LANES] + say_ref[...]
                    for i in range(0, span.shape[1], LANES)
                ],
                axis=1,
            ),
            first,
            across,
            out_ref,
        )


def step_kernel(last, others, span_ref, weight_ref, *refs):
    held, (out_ref, whole) = refs[:others], refs[others:]
    parts, rows = span_ref.shape[:2]
    comps, frames = whole.shape
    across, width = frames // LANES, frames // others
    for j in range(parts):
        down, along = j // across * rows, j % across * LANES
        whole[down : down + rows, along : along + LANES] = span_ref[j]
    span, sources = whole[...], frame_order(others)
    if span.dtype == jnp.bfloat16:
        gram = dot_rows(span, span)
    else:
        gram = lax.dot_general(
            span, span, ROWS_TO_ROWS, precision=EXACT, preferred_element_type=jnp.float32
        )
    chunk = weight_ref.shape[1]
    raw = jnp.zeros((comps, chunk), jnp.float32)
    for curves, source in zip(held, sources):
        part = whole[:, pl.ds(pl.multiple_of(source * width, LANES), width)]
        if span.dtype == jnp.bfloat16:
            raw = raw + dot_rows(part, mine(curves, chunk))
        else:
            raw = raw + fold(dot_rows(pieces(part), mine(curves, chunk)), comps)
    proj = solve_rows(gram, raw)
    if last:
        out_ref[...] = proj
    else:
        for span, first, across in span_of(proj, weight_ref[...], held, sources, out_ref):
            store_tiles(span, first, across, out_ref)


def place_kernel(own_ref, other_ref, out_ref, sems):
    frm = lax.axis_index("frm")
    copies = [
        pltpu.make_async_copy(own_ref, out_ref.at[frm], sems.at[0]),
        pltpu.make_async_copy(other_ref, out_ref.at[1 - frm], sems.at[1]),
    ]
    for copy in copies:
        copy.start()
    for copy in copies:
        copy.wait()


def add_and_give(annuli, in_ref, mark_ref, give_ref, out_ref):
    parts, rows = out_ref.shape[:2]

    def add(j, sums):
        part = in_ref[j].astype(jnp.float32)
        mark = mark_ref[pl.ds(j, 1), :]
        return tuple(s + jnp.where(mark == a, part, 0.0) for a, s in enumerate(sums))

    def give(j, sums):
        mark = give_ref[pl.ds(j, 1), :]
        total = sums[0]
        for a in range(1, annuli):
            total = jnp.where(mark == a, sums[a], total)
        out_ref[j] = total.astype(out_ref.dtype)
        return sums

    sums = tuple(jnp.zeros((rows, LANES), jnp.float32) for _ in range(annuli))
    if parts <= 32:
        for j in range(parts):
            sums = add(j, sums)
        for j in range(parts):
            give(j, sums)
    else:
        sums = lax.fori_loop(0, parts, add, sums)
        lax.fori_loop(0, parts, give, sums)


def first_sum_kernel(annuli, in_ref, mark_ref, out_ref, give_ref):
    for j in range(in_ref.shape[0]):
        label = mark_ref[j : j + 1, :]
        said = in_ref[j, :1, :].astype(jnp.int32)
        give_ref[j : j + 1, :] = jnp.where(label < 0, said, label)
    add_and_give(annuli, in_ref, mark_ref, give_ref, out_ref)


def sum_kernel(annuli, in_ref, give_ref, out_ref):
    add_and_give(annuli, in_ref, give_ref, give_ref, out_ref)


def shards(npix, nfrm, curves, annulus_of_block, ref_blocks, keep_mask, start_basis):
    pixels, width = curves.shape
    nblocks, block = keep_mask.shape
    annuli, comps, _ = start_basis.shape
    chunk, frames, parts = pixels // nfrm, width * nfrm, npix * nfrm
    rows = comps * frames // LANES // parts
    narrow = jnp.bfloat16 if rows % 16 == 0 else jnp.float32

    labels = annulus_of_block.reshape(1, nblocks)
    vmem = pl.BlockSpec(memory_space=pltpu.VMEM)
    hbm = pl.BlockSpec(memory_space=pltpu.HBM)
    shape = jax.ShapeDtypeStruct

    def call(kernel, out, ins, outs, name, scratch=(), mib=32):
        return pl.pallas_call(
            kernel,
            out_shape=out,
            in_specs=ins,
            out_specs=outs,
            scratch_shapes=list(scratch),
            compiler_params=pltpu.CompilerParams(vmem_limit_bytes=mib * 1024 * 1024),
            name=name,
        )

    def rotate(x, shift):
        return lax.ppermute(x, "frm", [(i, (i + shift) % nfrm) for i in range(nfrm)])

    messages = call(
        pack_kernel,
        [shape((chunk, width), jnp.bfloat16)] * (nfrm - 1),
        [hbm],
        [vmem] * (nfrm - 1),
        "pack",
        [pltpu.SemaphoreType.DMA((nfrm - 1,))],
    )(curves)
    got = [rotate(message, shift) for shift, message in enumerate(messages, 1)]
    picks = call(
        functools.partial(pick_kernel, block, chunk),
        [shape((comps, width), jnp.bfloat16)] * (nfrm - 1),
        [vmem, vmem],
        [vmem] * (nfrm - 1),
        "pick",
    )(labels, start_basis)
    starts = [rotate(pick, shift) for shift, pick in enumerate(picks, 1)]
    raw, weight, say, marks = call(
        functools.partial(own_kernel, block, nfrm),
        (
            shape((comps, chunk), jnp.float32),
            shape((1, chunk), jnp.float32),
            shape((1, LANES), jnp.float32),
            shape((parts, LANES), jnp.int32),
        ),
        [vmem] * 5,
        (vmem, vmem, vmem, vmem),
        "own_part",
    )(labels, ref_blocks, keep_mask.reshape(nfrm, chunk), curves, start_basis)
    held = [curves, *got]
    sent = call(
        functools.partial(first_kernel, nfrm),
        shape((parts, rows, LANES), jnp.float32),
        [vmem] * (4 + 2 * (nfrm - 1)),
        vmem,
        "first_span",
    )(raw, weight, say, curves, *got, *starts)

    give = None
    for step in range(ITERS):
        kind = narrow if step else jnp.float32
        taken = lax.all_to_all(sent, BOTH, 0, 0, tiled=True)
        total = shape((parts, rows, LANES), kind)
        if step == 0:
            total, give = call(
                functools.partial(first_sum_kernel, annuli),
                (total, shape((parts, LANES), jnp.int32)),
                [vmem, vmem],
                (vmem, vmem),
                "first_sum",
            )(taken, marks)
        else:
            total = call(
                functools.partial(sum_kernel, annuli), total, [vmem, vmem], vmem, "sum"
            )(taken, give)
        span = lax.all_to_all(total, BOTH, 0, 0, tiled=True)
        last = step == ITERS - 1
        sent = call(
            functools.partial(step_kernel, last, nfrm),
            shape((comps, chunk), jnp.float32) if last else shape((parts, rows, LANES), narrow),
            [vmem] * (2 + nfrm),
            vmem,
            "fit" if last else "step",
            [pltpu.VMEM((comps, frames), kind)],
        )(span, weight, *held)

    if nfrm == 2 and chunk == block:
        return call(
            place_kernel,
            shape((nblocks, comps, chunk), jnp.float32),
            [vmem, vmem],
            hbm,
            "place",
            [pltpu.SemaphoreType.DMA((2,))],
        )(sent, rotate(sent, 1))
    every = lax.all_gather(sent, "frm")
    return every.swapaxes(0, 1).reshape(comps, nblocks, block).swapaxes(0, 1)


def solution(mesh):
    in_specs = (P("pix", "frm"), P("pix"), P(), P("pix", None), P(None, None, "frm"))
    out_specs = P("pix", None, None)
    body = functools.partial(shards, mesh.shape["pix"], mesh.shape["frm"])
    return jax.shard_map(body, mesh=mesh, in_specs=in_specs, out_specs=out_specs, check_vma=False)
```

```python
import functools

import jax
import jax.numpy as jnp
from jax import lax
from jax.experimental import pallas as pl
from jax.experimental.pallas import tpu as pltpu
from jax.sharding import PartitionSpec as P

ITERS = 4
LANES = 128
PANEL = 16
BOTH = ("frm", "pix")
EXACT = lax.Precision.HIGHEST
ROWS_TO_ROWS = (((1,), (1,)), ((), ()))


def solve_rows(gram, raw):
    k = gram.shape[0]
    rows = lax.broadcasted_iota(jnp.int32, (k, LANES), 0)
    low = jnp.concatenate([gram, jnp.zeros((k, LANES - k), jnp.float32)], axis=1)
    wide = raw.shape[1] // LANES if raw.shape[1] % LANES == 0 else 1
    size = raw.shape[1] // wide
    right = [raw[:, t * size : (t + 1) * size] for t in range(wide)]
    done = [[] for _ in right]
    pivots = jnp.zeros((k, LANES), jnp.float32)
    for base in range(0, k, PANEL):
        below = rows[base:, :]
        panel = [jnp.broadcast_to(low[:, base + j : base + j + 1], low.shape) for j in range(PANEL)]
        pivot = panel[0][:1, :]
        for j in range(PANEL):
            inverse = 1.0 / pivot
            pivots = jnp.where(rows == base + j, pivot, pivots)
            if j + 1 < PANEL:
                beside = panel[j + 1][j : j + 1, :]
                pivot = panel[j + 1][j + 1 : j + 2, :] - beside * beside * inverse
            factor = jnp.where(below > base + j, panel[j] * inverse, 0.0)
            for i in range(j + 1, PANEL):
                panel[i] = panel[i] - factor * panel[i][j : j + 1, :]
            if base + PANEL < k:
                low = low - factor * low[j : j + 1, :]
            right = [x - factor[:, :size] * x[j : j + 1, :] for x in right]
        low = low[PANEL:, :]
        for held, x in zip(done, right):
            held.append(x[:PANEL, :])
        right = [x[PANEL:, :] for x in right]
    scale = lax.rsqrt(pivots)[:, :size]
    return jnp.concatenate([jnp.concatenate(held, axis=0) * scale for held in done], axis=1)


def pieces(wide):
    high = wide.astype(jnp.bfloat16)
    rest = wide - high.astype(jnp.float32)
    middle = rest.astype(jnp.bfloat16)
    low = (rest - middle.astype(jnp.float32)).astype(jnp.bfloat16)
    return jnp.concatenate([high, middle, low], axis=0)


def fold(stacked, k):
    return (stacked[2 * k :] + stacked[k : 2 * k]) + stacked[:k]


def dot_rows(left, right):
    return lax.dot_general(left, right, ROWS_TO_ROWS, preferred_element_type=jnp.float32)


def store_tiles(span, first, across, out_ref):
    rows = out_ref.shape[1]
    for down in range(span.shape[0] // rows):
        for along in range(span.shape[1] // LANES):
            tile = span[down * rows : (down + 1) * rows, along * LANES : (along + 1) * LANES]
            out_ref[first + (down * across + along)] = tile.astype(out_ref.dtype)


def mine(curves, chunk):
    if curves.shape[0] == chunk:
        return curves[...]
    return curves[pl.ds(pl.multiple_of(lax.axis_index("frm") * chunk, chunk), chunk), :]


def span_of(proj, weight, held, sources, out_ref):
    proj_bf = (proj * weight).astype(jnp.bfloat16)
    width = held[0].shape[1] // LANES
    for curves, source in zip(held, sources):
        span = jnp.dot(proj_bf, mine(curves, proj.shape[1]), preferred_element_type=jnp.float32)
        yield span, source * width, width * len(held)


def frame_order(others):
    frm = lax.axis_index("frm")
    return [lax.rem(frm - shift + others, others) for shift in range(others)]


def pack_kernel(own_ref, *refs):
    out_refs, sems = refs[:-1], refs[-1]
    others = len(out_refs) + 1
    chunk = out_refs[0].shape[0]
    copies = []
    for shift, out_ref in enumerate(out_refs, 1):
        target = lax.rem(lax.axis_index("frm") + shift, others)
        rows = pl.ds(pl.multiple_of(target * chunk, chunk), chunk)
        copies.append(pltpu.make_async_copy(own_ref.at[rows], out_ref, sems.at[shift - 1]))
    for copy in copies:
        copy.start()
    for copy in copies:
        copy.wait()


def entry(row_ref, at):
    lanes = lax.broadcasted_iota(jnp.int32, row_ref.shape, 1)
    return jnp.sum(jnp.where(lanes == at, row_ref[...], 0).astype(jnp.float32)).astype(jnp.int32)


def pick_kernel(block, chunk, ann_ref, start_ref, *out_refs):
    others = len(out_refs) + 1
    for shift, out_ref in enumerate(out_refs, 1):
        target = lax.rem(lax.axis_index("frm") + shift, others)
        out_ref[...] = start_ref[entry(ann_ref, target * chunk // block)]


def own_kernel(
    block, others, ann_ref, listed_ref, keep_ref, own_ref, start_ref,
    raw_ref, weight_ref, say_ref, mark_ref,
):
    pix, frm = lax.axis_index("pix"), lax.axis_index("frm")
    chunk = raw_ref.shape[1]
    label = entry(ann_ref, frm * chunk // block)
    raw_ref[...] = dot_rows(start_ref[label], mine(own_ref, chunk))
    npix = mark_ref.shape[0] // others
    place = lax.broadcasted_iota(jnp.int32, (mark_ref.shape[0], LANES), 0)
    blocks = place % npix * ann_ref.shape[1] + place // npix * chunk // block
    marks = jnp.full(place.shape, -1, jnp.int32)
    for a in range(listed_ref.shape[0]):
        for at in range(listed_ref.shape[1]):
            marks = jnp.where(blocks == listed_ref[a : a + 1, at : at + 1], a, marks)
    for j in range(mark_ref.shape[0]):
        mark_ref[j] = jnp.broadcast_to(marks[j : j + 1, :], mark_ref.shape[1:])
    listed = mark_ref[frm * npix + pix][:1, :] >= 0
    kept = keep_ref[pl.ds(frm, 1), :]
    weight_ref[...] = jnp.where((kept == 1) & listed[:, :1], 1.0, 0.0)
    say_ref[...] = jnp.where(listed, 0, label).astype(jnp.float32)


def first_kernel(others, raw_ref, weight_ref, say_ref, own_ref, *refs):
    got, starts, out_ref = refs[: others - 1], refs[others - 1 : -1], refs[-1]
    proj = raw_ref[...]
    for curves, start in zip(got, starts):
        proj = proj + dot_rows(start[...], curves[...])
    held, weight = (own_ref, *got), weight_ref[...]
    for span, first, across in span_of(proj, weight, held, frame_order(others), out_ref):
        store_tiles(
            jnp.concatenate(
                [
                    span[:, i : i + LANES] + say_ref[...]
                    for i in range(0, span.shape[1], LANES)
                ],
                axis=1,
            ),
            first,
            across,
            out_ref,
        )


def step_kernel(last, others, span_ref, weight_ref, *refs):
    held, (out_ref, whole) = refs[:others], refs[others:]
    parts, rows = span_ref.shape[:2]
    comps, frames = whole.shape
    across, width = frames // LANES, frames // others
    for j in range(parts):
        down, along = j // across * rows, j % across * LANES
        whole[down : down + rows, along : along + LANES] = span_ref[j]
    span, sources = whole[...], frame_order(others)
    if span.dtype == jnp.bfloat16:
        gram = dot_rows(span, span)
    else:
        gram = lax.dot_general(
            span, span, ROWS_TO_ROWS, precision=EXACT, preferred_element_type=jnp.float32
        )
    chunk = weight_ref.shape[1]
    raw = jnp.zeros((comps, chunk), jnp.float32)
    for curves, source in zip(held, sources):
        part = whole[:, pl.ds(pl.multiple_of(source * width, LANES), width)]
        if span.dtype == jnp.bfloat16:
            raw = raw + dot_rows(part, mine(curves, chunk))
        else:
            raw = raw + fold(dot_rows(pieces(part), mine(curves, chunk)), comps)
    proj = solve_rows(gram, raw)
    if last:
        out_ref[...] = proj
    else:
        for span, first, across in span_of(proj, weight_ref[...], held, sources, out_ref):
            store_tiles(span, first, across, out_ref)


def place_kernel(own_ref, other_ref, out_ref, sems):
    frm = lax.axis_index("frm")
    copies = [
        pltpu.make_async_copy(own_ref, out_ref.at[frm], sems.at[0]),
        pltpu.make_async_copy(other_ref, out_ref.at[1 - frm], sems.at[1]),
    ]
    for copy in copies:
        copy.start()
    for copy in copies:
        copy.wait()


def add_and_give(annuli, in_ref, mark_ref, give_ref, out_ref):
    parts, rows = out_ref.shape[:2]

    def over(ref, j):
        return jnp.concatenate([ref[j]] * (rows // ref.shape[1]), axis=0)

    def add(j, sums):
        part, mark = in_ref[j].astype(jnp.float32), over(mark_ref, j)
        return tuple(s + jnp.where(mark == a, part, 0.0) for a, s in enumerate(sums))

    def give(j, sums):
        mark, total = over(give_ref, j), sums[0]
        for a in range(1, annuli):
            total = jnp.where(mark == a, sums[a], total)
        out_ref[j] = total.astype(out_ref.dtype)
        return sums

    sums = tuple(jnp.zeros((rows, LANES), jnp.float32) for _ in range(annuli))
    if parts <= 32:
        for j in range(parts):
            sums = add(j, sums)
        for j in range(parts):
            give(j, sums)
    else:
        sums = lax.fori_loop(0, parts, add, sums)
        lax.fori_loop(0, parts, give, sums)


def first_sum_kernel(annuli, in_ref, mark_ref, out_ref, give_ref):
    for j in range(in_ref.shape[0]):
        label, said = mark_ref[j], in_ref[j, :1, :].astype(jnp.int32)
        give_ref[j] = jnp.where(label < 0, jnp.broadcast_to(said, label.shape), label)
    add_and_give(annuli, in_ref, mark_ref, give_ref, out_ref)


def sum_kernel(annuli, in_ref, give_ref, out_ref):
    add_and_give(annuli, in_ref, give_ref, give_ref, out_ref)


def shards(npix, nfrm, curves, annulus_of_block, ref_blocks, keep_mask, start_basis):
    pixels, width = curves.shape
    nblocks, block = keep_mask.shape
    annuli, comps, _ = start_basis.shape
    chunk, frames, parts = pixels // nfrm, width * nfrm, npix * nfrm
    rows = comps * frames // LANES // parts
    narrow = jnp.bfloat16 if rows % 16 == 0 else jnp.float32

    labels = annulus_of_block.reshape(1, nblocks)
    vmem = pl.BlockSpec(memory_space=pltpu.VMEM)
    hbm = pl.BlockSpec(memory_space=pltpu.HBM)
    shape = jax.ShapeDtypeStruct
    table = shape((parts, min(rows, 8), LANES), jnp.int32)

    def call(kernel, out, ins, outs, name, scratch=(), mib=32):
        return pl.pallas_call(
            kernel,
            out_shape=out,
            in_specs=ins,
            out_specs=outs,
            scratch_shapes=list(scratch),
            compiler_params=pltpu.CompilerParams(vmem_limit_bytes=mib * 1024 * 1024),
            name=name,
        )

    def rotate(x, shift):
        return lax.ppermute(x, "frm", [(i, (i + shift) % nfrm) for i in range(nfrm)])

    messages = call(
        pack_kernel,
        [shape((chunk, width), jnp.bfloat16)] * (nfrm - 1),
        [hbm],
        [vmem] * (nfrm - 1),
        "pack",
        [pltpu.SemaphoreType.DMA((nfrm - 1,))],
    )(curves)
    got = [rotate(message, shift) for shift, message in enumerate(messages, 1)]
    picks = call(
        functools.partial(pick_kernel, block, chunk),
        [shape((comps, width), jnp.bfloat16)] * (nfrm - 1),
        [vmem, vmem],
        [vmem] * (nfrm - 1),
        "pick",
    )(labels, start_basis)
    starts = [rotate(pick, shift) for shift, pick in enumerate(picks, 1)]
    raw, weight, say, marks = call(
        functools.partial(own_kernel, block, nfrm),
        (
            shape((comps, chunk), jnp.float32),
            shape((1, chunk), jnp.float32),
            shape((1, LANES), jnp.float32),
            table,
        ),
        [vmem] * 5,
        (vmem, vmem, vmem, vmem),
        "own_part",
    )(labels, ref_blocks, keep_mask.reshape(nfrm, chunk), curves, start_basis)
    held = [curves, *got]
    sent = call(
        functools.partial(first_kernel, nfrm),
        shape((parts, rows, LANES), jnp.float32),
        [vmem] * (4 + 2 * (nfrm - 1)),
        vmem,
        "first_span",
    )(raw, weight, say, curves, *got, *starts)

    give = None
    for step in range(ITERS):
        kind = narrow if step else jnp.float32
        taken = lax.all_to_all(sent, BOTH, 0, 0, tiled=True)
        total = shape((parts, rows, LANES), kind)
        if step == 0:
            total, give = call(
                functools.partial(first_sum_kernel, annuli),
                (total, table),
                [vmem, vmem],
                (vmem, vmem),
                "first_sum",
            )(taken, marks)
        else:
            total = call(
                functools.partial(sum_kernel, annuli), total, [vmem, vmem], vmem, "sum"
            )(taken, give)
        span = lax.all_to_all(total, BOTH, 0, 0, tiled=True)
        last = step == ITERS - 1
        sent = call(
            functools.partial(step_kernel, last, nfrm),
            shape((comps, chunk), jnp.float32) if last else shape((parts, rows, LANES), narrow),
            [vmem] * (2 + nfrm),
            vmem,
            "fit" if last else "step",
            [pltpu.VMEM((comps, frames), kind)],
        )(span, weight, *held)

    if nfrm == 2 and chunk == block:
        return call(
            place_kernel,
            shape((nblocks, comps, chunk), jnp.float32),
            [vmem, vmem],
            hbm,
            "place",
            [pltpu.SemaphoreType.DMA((2,))],
        )(sent, rotate(sent, 1))
    every = lax.all_gather(sent, "frm")
    return every.swapaxes(0, 1).reshape(comps, nblocks, block).swapaxes(0, 1)


def solution(mesh):
    in_specs = (P("pix", "frm"), P("pix"), P(), P("pix", None), P(None, None, "frm"))
    out_specs = P("pix", None, None)
    body = functools.partial(shards, mesh.shape["pix"], mesh.shape["frm"])
    return jax.shard_map(body, mesh=mesh, in_specs=in_specs, out_specs=out_specs, check_vma=False)
```
